256 devices in a mesh: layer: 4 (over x), row: 8 (over z), col: 8 (over y, core).
Axes of the slice: x: 4, y: 4, z: 8, core: 2. Of those that a mesh axis runs over, the one named last changes fastest.
Arguments:
- a_values: bfloat16 [8, 32, 24, 128, 128], P('row', ('layer', 'col')), may hold values from -6 to 6
- a_rows: int32 [8, 32, 24], P('row', ('layer', 'col')), may hold values from 0 to 3, as said below
- a_ks: int32 [8, 32, 24], P('row', ('layer', 'col')), may hold values from 0 to 31
- a_count: int32 [32, 8], P(('layer', 'col'), 'row'), may hold values from 1 to 24, 64 in all within a row
- t_panel: bfloat16 [131072, 2048], P(('layer', 'col'), 'row'), may hold values from -0.0625 to 0.0625
Outputs:
- next_sign: bfloat16 [4096, 2048], P(('layer', 'col'), 'row')
The draws below stay inside these ranges and needn't reach their ends.
Inputs may be any that keep to these rules, and one draw needn't show every extreme that they name: Within one device's 24 slots the pairs (a_rows, a_ks) are all different. `a_count`: for every inner panel the 8 counts sum to exactly 64, and one of them is exactly 24.
All inputs are finite; a program needn't handle non-finite values. No bound on the sum of `a_count` on one device may be relied on, other than what follows from the above.
Results may differ from the reference program's by a relative error of at most 0.001.
Values may be sent and summed in bfloat16 or wider, within the bound.
A program may use at most 128 MiB of HBM per device.

```python
import math
import jax
import jax.numpy as jnp
import numpy as np
from jax import lax

BLK = 128
NB = 1024
RB = 4
CR = 2
BAL = 8
SA = 24
KS = 32
N_LAYER = 4
N_ROW = 8
N_COL = 8


def block_places(key):
    keys = jax.random.split(key, N_ROW * N_LAYER * N_COL)
    places = jax.vmap(lambda single: jax.random.permutation(single, RB * KS)[:SA])(keys)
    return places.reshape(N_ROW, N_LAYER * N_COL, SA).astype(jnp.int32)


def draw_a_rows(key, part):
    places = block_places(key)
    return (places // KS).astype(jnp.int32)


def draw_a_ks(key, part):
    places = block_places(key)
    return (places % KS).astype(jnp.int32)


def steps_of(stream_key, dims, cuts, low, largest):
    gain, own = 1.0, jax.random.fold_in(stream_key, 6)
    for axis_at, blocks in cuts:
        draws = jnp.exp(jax.random.uniform(jax.random.fold_in(own, axis_at), (blocks,), jnp.float32, low / len(cuts), largest / len(cuts)))
        gain = gain * jnp.repeat(draws, dims[axis_at] // blocks).reshape([-1 if axis == axis_at else 1 for axis in range(len(dims))])
    return gain


def split_up(amount, total, reach, slope):
    loads = [(1 << 20) // math.isqrt(rank ** slope) + 1 for rank in range(2, amount + 1)]
    surplus, given = total - reach - (amount - 1), [1] * (amount - 1)
    while surplus > 0:
        free = [i for i in range(amount - 1) if given[i] < reach]
        mass, budget = sum([loads[i] for i in free]), surplus
        for i in free:
            more = min(reach - given[i], max(1, budget * loads[i] // mass), surplus)
            given[i] = given[i] + more
            surplus = surplus - more
    return np.array([reach] + given)


def ragged_sizes(stream_key, count, total, most, lean):
    if count == 2:
        one = jax.random.randint(stream_key, (), max(1, total - most), min(most, total - 1) + 1)
        return jnp.stack([one, total - one])
    tallies = jnp.asarray(split_up(count, total, most, lean), jnp.int32)
    pairs = (count - 1) // 2
    giver, receiver = tallies[1:1 + 2 * pairs:2], tallies[2:2 + 2 * pairs:2]
    room = jnp.minimum(giver - 1, most - receiver)
    passed = jax.random.randint(jax.random.fold_in(stream_key, 1), (pairs,), 0, 1 << 20) % (room + 1)
    tallies = tallies.at[1:1 + 2 * pairs:2].set(giver - passed).at[2:2 + 2 * pairs:2].set(receiver + passed)
    return tallies[jax.random.permutation(jax.random.fold_in(stream_key, 2), count)]


def centred(rng, shape, width, reach, shards=(), held_as=jnp.bfloat16):
    result = width * jax.random.normal(rng, shape, jnp.float32)
    if shards:
        result = result * steps_of(rng, shape, shards, -0.22, 0.18)
    return jnp.clip(result, -reach, reach).astype(held_as)


def setup_inputs(seed: int = 0) -> dict:
    streams_of = jax.random.split(jax.random.key(seed), 6)
    a_values = centred(streams_of[0], (N_ROW, N_LAYER * N_COL, SA, BLK, BLK), 1.0, 6.0, ((0, 8), (1, 32)))
    a_rows = draw_a_rows(jax.random.fold_in(streams_of[5], 71), 0)
    a_ks = draw_a_ks(jax.random.fold_in(streams_of[5], 71), 0)
    a_count = jax.vmap(lambda own: ragged_sizes(own, N_ROW, BAL * N_ROW, SA, 2))(jax.random.split(streams_of[3], (N_LAYER * N_COL))).reshape((N_LAYER * N_COL, N_ROW)).astype(jnp.int32)
    t_panel = centred(streams_of[4], (NB * BLK, N_ROW * CR * BLK), (BLK * N_LAYER * N_COL * BAL // RB) ** -0.5, 0.0625, ((0, 32), (1, 8)))
    return dict(a_values=a_values, a_rows=a_rows, a_ks=a_ks, a_count=a_count, t_panel=t_panel)


def reference(a_values, a_rows, a_ks, a_count, t_panel):
    panel_width = t_panel.shape[1]
    live_total = N_ROW * BAL
    strips = t_panel.reshape(N_LAYER * N_COL, KS, BLK, panel_width)
    place = jnp.arange(live_total, dtype=jnp.int32)

    def one_panel(partial_value, panel):
        counts = a_count[panel].astype(jnp.int32)
        starts = (jnp.cumsum(counts) - counts).astype(jnp.int32)
        owner_row = (jnp.sum((place[:, None] >= starts[None, :]).astype(jnp.int32), axis=1) - 1).astype(jnp.int32)
        within = (place - starts[owner_row]).astype(jnp.int32)
        block_values = a_values[owner_row, panel, within].astype(jnp.float32)
        block_rows = (owner_row * RB + a_rows[owner_row, panel, within]).astype(jnp.int32)
        block_inner = a_ks[owner_row, panel, within].astype(jnp.int32)
        chosen = strips[panel][block_inner].astype(jnp.float32)
        product = jnp.einsum('pmk,pkn->pmn', block_values, chosen)
        return partial_value.at[block_rows].add(product), None

    partial_value, _ = lax.scan(one_panel, jnp.zeros((N_ROW * RB, BLK, panel_width), jnp.float32), jnp.arange(N_LAYER * N_COL, dtype=jnp.int32))
    return (0.5 * partial_value.reshape(N_ROW * RB * BLK, panel_width)).astype(jnp.bfloat16)
```

```python
import functools

import jax
import jax.numpy as jnp
from jax import lax
from jax.experimental import pallas as pl
from jax.experimental.pallas import tpu as pltpu
from jax.sharding import PartitionSpec as P

MESH = pl.DeviceIdType.MESH
RB = 4
CH = 4


def kernel(dims, a_ref, rows_ref, ks_ref, count_ref, t_ref, out_ref,
           t_v, rxa, cmp_v, ring, meta, meta_all, tab, tab_s, run,
           mine, to_core, from_core, total, from_chip,
           loc_sem, a_send, a_recv, m_send, m_recv, g_send, g_recv, c_send, c_recv, x_send, x_recv):
    nx, nz, ny, slots, blk, live = dims
    chips = nx * ny
    sub = blk // nz
    blocks = nz * RB
    lx, rz, co = lax.axis_index("layer"), lax.axis_index("row"), lax.axis_index("col")
    cy, core = lax.div(co, 2), lax.rem(co, 2)
    chip = lx * ny + cy

    def on_z(o):
        return (lx, lax.rem(rz + o + nz, nz), co)

    def on_plane(q):
        dx, dy = lax.div(q, ny), lax.rem(q, ny)
        return lax.rem(lx + dx, nx), lax.rem(cy + dy, ny)

    def plane_device(q):
        x, y = on_plane(q)
        return (x, rz, 2 * y + core)

    other_core = (lx, rz, 2 * cy + 1 - core)

    t_copy = pltpu.make_async_copy(t_ref, t_v, loc_sem.at[0])
    t_copy.start()
    own_piece = pltpu.make_async_copy(
        a_ref.at[:, pl.ds(pl.multiple_of(rz * sub, sub), sub), :], rxa.at[pl.ds(rz * slots, slots)], loc_sem.at[1])
    own_piece.start()

    barrier = pltpu.get_barrier_semaphore()

    def greet_z(o, c_):
        pl.semaphore_signal(barrier, inc=1, device_id=on_z(o), device_id_type=MESH)
        return c_

    def greet_plane(q, c_):
        pl.semaphore_signal(barrier, inc=1, device_id=plane_device(q), device_id_type=MESH)
        return c_

    lax.fori_loop(1, nz, greet_z, 0)
    pl.semaphore_signal(barrier, inc=1, device_id=other_core, device_id_type=MESH)
    lax.fori_loop(1, chips, greet_plane, 0)

    meta[...] = jnp.zeros_like(meta)
    meta[0:1, 0:slots] = rows_ref[0]
    meta[1:2, 0:slots] = ks_ref[0]
    meta[2:3, :] = jnp.broadcast_to(count_ref[...], (1, 128))

    pl.semaphore_wait(barrier, nz - 1 + 1 + chips - 1)

    def a_copy(o):
        to = lax.rem(rz + o, nz)
        return pltpu.make_async_remote_copy(
            src_ref=a_ref.at[:, pl.ds(pl.multiple_of(to * sub, sub), sub), :],
            dst_ref=rxa.at[pl.ds(rz * slots, slots)],
            send_sem=a_send.at[o], recv_sem=a_recv.at[o], device_id=on_z(o), device_id_type=MESH)

    def m_copy(o):
        return pltpu.make_async_remote_copy(
            src_ref=meta, dst_ref=meta_all.at[rz],
            send_sem=m_send.at[o], recv_sem=m_recv.at[o], device_id=on_z(o), device_id_type=MESH)

    def a_arrived(o):
        source = lax.rem(rz - o + nz, nz)
        return pltpu.make_async_remote_copy(
            src_ref=a_ref.at[:, pl.ds(0, sub), :], dst_ref=rxa.at[pl.ds(source * slots, slots)],
            send_sem=a_send.at[o], recv_sem=a_recv.at[o], device_id=on_z(o), device_id_type=MESH)

    def m_arrived(o):
        source = lax.rem(rz - o + nz, nz)
        return pltpu.make_async_remote_copy(
            src_ref=meta, dst_ref=meta_all.at[source],
            send_sem=m_send.at[o], recv_sem=m_recv.at[o], device_id=on_z(o), device_id_type=MESH)

    def start_meta(o, c_):
        m_copy(o).start()
        return c_

    def start_pieces(o, c_):
        a_copy(o).start()
        return c_

    lax.fori_loop(1, nz, start_meta, 0)
    lax.fori_loop(1, nz, start_pieces, 0)

    meta_all[pl.ds(rz, 1)] = meta[...][None]

    def wait_meta(o, c_):
        m_arrived(o).wait_recv()
        m_copy(o).wait_send()
        return c_

    lax.fori_loop(1, nz, wait_meta, 0)

    row_of, col_of, count_of = meta_all[:, 0, :], meta_all[:, 1, :], meta_all[:, 2, :]
    lane = lax.broadcasted_iota(jnp.int32, (nz, 128), 1)
    group = lax.broadcasted_iota(jnp.int32, (nz, 128), 0)
    alive = lane < count_of
    row_key = jnp.where(alive, row_of, RB)
    rank = jnp.zeros((nz, 128), jnp.int32)
    in_row = jnp.zeros((nz, 128), jnp.int32)
    for g in range(nz - 1):
        rank = rank + jnp.where(group > g, jnp.broadcast_to(count_of[g:g + 1, :], (nz, 128)), 0)
    for s in range(slots):
        key = jnp.broadcast_to(row_key[:, s:s + 1], (nz, 128))
        same_before = jnp.where((key == row_key) & (lane > s), 1, 0)
        in_row = in_row + same_before
        rank = rank + same_before + jnp.where(key < row_key, 1, 0)
    rank = jnp.where(alive, rank, 1000)
    slot_at = jnp.zeros((nz, 128), jnp.int32)
    col_at = jnp.zeros((nz, 128), jnp.int32)
    keep_at = jnp.zeros((nz, 128), jnp.int32)
    upto = jnp.zeros((nz, 128), jnp.int32)
    equal = jnp.zeros((nz, 128), jnp.int32)
    for s in range(slots):
        hit = jnp.broadcast_to(rank[:, s:s + 1], (nz, 128)) == lane
        slot_at = slot_at + jnp.where(hit, group * slots + s, 0)
        col_at = col_at + jnp.where(hit, jnp.broadcast_to(col_of[:, s:s + 1], (nz, 128)), 0)
        keep_at = keep_at + jnp.where(hit, jnp.broadcast_to(in_row[:, s:s + 1], (nz, 128)), 0)
        key = jnp.broadcast_to(row_key[:, s:s + 1], (nz, 128))
        full_key = jnp.where(key < RB, group * RB + key, 1000)
        upto = upto + jnp.where(full_key <= lane, 1, 0)
        equal = equal + jnp.where(full_key == lane, 1, 0)
    last_at = jnp.sum(upto, axis=0, keepdims=True) - 1
    tab[0:1, :] = jnp.sum(slot_at, axis=0, keepdims=True)
    tab[1:2, :] = jnp.sum(col_at, axis=0, keepdims=True)
    tab[2:3, :] = jnp.sum(keep_at, axis=0, keepdims=True)
    tab[3:4, :] = jnp.where(jnp.sum(equal, axis=0, keepdims=True) > 0, last_at, live)
    tab[4:8, :] = jnp.zeros((4, 128), jnp.int32)
    table = pltpu.make_async_copy(tab, tab_s, loc_sem.at[2])
    table.start()
    run[live] = jnp.zeros(run.shape[1:], jnp.float32)
    table.wait()
    t_copy.wait()
    own_piece.wait()

    def wait_pieces(o, c_):
        a_arrived(o).wait_recv()
        a_copy(o).wait_send()
        return c_

    lax.fori_loop(1, nz, wait_pieces, 0)

    def compact(m, c_):
        cmp_v[m] = rxa[tab_s[0, m]]
        return c_

    lax.fori_loop(0, live, compact, 0, unroll=8)

    cs = live // CH

    def ring_copy(d, hop, c):
        src = cmp_v if hop == 1 else ring.at[3 * d + hop - 2]
        dst = ring.at[6] if hop == 4 else ring.at[3 * d + hop - 1]
        return pltpu.make_async_remote_copy(
            src_ref=src.at[pl.ds(cs * c, cs)], dst_ref=dst.at[pl.ds(cs * c, cs)],
            send_sem=g_send.at[d, hop - 1, c], recv_sem=g_recv.at[d, hop - 1, c],
            device_id=on_z(1 - 2 * d), device_id_type=MESH)

    def last_hop_chunk(d, c):
        return (c < CH // 2) == (d == 0)

    for c in range(CH):
        for d in (0, 1):
            ring_copy(d, 1, c).start()

    def multiply(pieces, c, carry):
        def item(i, acc):
            b = c * cs + i
            lhs = pieces[0][b] if len(pieces) == 1 else jnp.concatenate([p[b] for p in pieces], axis=0)
            term = jnp.dot(lhs, t_v[tab_s[1, b]], preferred_element_type=jnp.float32)
            acc = jnp.where(tab_s[2, b] > 0, acc, 0.0) + term
            run[b, 0:acc.shape[0]] = acc
            return acc
        return lax.fori_loop(0, cs, item, carry, unroll=8)

    def rows_in(t):
        return sub if t in (0, 4) else 2 * sub

    def core_copy(t):
        n = rows_in(t)
        return pltpu.make_async_remote_copy(
            src_ref=to_core.at[t, :, pl.ds(0, n)], dst_ref=from_core.at[t, :, pl.ds(0, n)],
            send_sem=c_send.at[t], recv_sem=c_recv.at[t], device_id=other_core, device_id_type=MESH)

    def split_rows(t):
        n = rows_in(t)

        def one(r, c_):
            mine[t, r, 0:n] = run[tab_s[3, 2 * r + core], 0:n]
            to_core[t, r, 0:n] = run[tab_s[3, 2 * r + 1 - core], 0:n]
            return c_

        lax.fori_loop(0, blocks // 2, one, 0, unroll=4)
        core_copy(t).start()

    def chip_copy(t, q):
        n = rows_in(t)
        x, y = on_plane(q)
        return pltpu.make_async_remote_copy(
            src_ref=total.at[t, x * ny + y, pl.ds(0, n)], dst_ref=from_chip.at[t, q, pl.ds(0, n)],
            send_sem=x_send.at[t, q], recv_sem=x_recv.at[t, q], device_id=(x, rz, 2 * y + core), device_id_type=MESH)

    def send_rows(t):
        n = rows_in(t)
        core_copy(t).wait_recv()

        def one(r, c_):
            total[t, r, 0:n] = mine[t, r, 0:n] + from_core[t, r, 0:n]
            return c_

        lax.fori_loop(0, chips, one, 0, unroll=4)

        def send(q, c_):
            chip_copy(t, q).start()
            return c_

        lax.fori_loop(1, chips, send, 0)

    def finish(t):
        n = rows_in(t)

        def wait(q, c_):
            chip_copy(t, q).wait_recv()
            return c_

        lax.fori_loop(1, chips, wait, 0)

        def add(q, acc):
            return acc + from_chip[t, q, 0:n]

        acc = lax.fori_loop(1, chips, add, total[t, chip, 0:n], unroll=5)
        acc = (0.5 * acc).astype(out_ref.dtype)
        for k in range(n // sub):
            shift = 0 if t == 0 else (t if k else nz - t)
            piece = lax.rem(rz + shift, nz)
            out_ref[pl.ds(pl.multiple_of(piece * sub, sub), sub), :] = acc[k * sub:(k + 1) * sub]

    width = t_v.shape[2]
    acc = jnp.zeros((sub, width), jnp.float32)
    for c in range(CH):
        acc = multiply([cmp_v], c, acc)
    split_rows(0)
    for t in (1, 2, 3):
        acc = jnp.zeros((2 * sub, width), jnp.float32)
        for c in range(CH):
            for d in (0, 1):
                ring_copy(d, t, c).wait_recv()
                if t < 3 or last_hop_chunk(d, c):
                    ring_copy(d, t + 1, c).start()
            acc = multiply([ring.at[t - 1], ring.at[3 + t - 1]], c, acc)
            if c == 1:
                send_rows(t - 1)
        split_rows(t)
    acc = jnp.zeros((sub, width), jnp.float32)
    for c in range(CH):
        ring_copy(0 if last_hop_chunk(0, c) else 1, 4, c).wait_recv()
        acc = multiply([ring.at[6]], c, acc)
        if c == 1:
            send_rows(3)
    split_rows(4)
    for t in (0, 1, 2):
        finish(t)
    send_rows(4)
    finish(3)
    finish(4)

    for d in (0, 1):
        for hop in (1, 2, 3, 4):
            for c in range(CH):
                if hop < 4 or last_hop_chunk(d, c):
                    ring_copy(d, hop, c).wait_send()
    for t in range(5):
        core_copy(t).wait_send()

        def sent(q, c_):
            chip_copy(t, q).wait_send()
            return c_

        lax.fori_loop(1, chips, sent, 0)


def shards(nx, nz, ny, a_values, a_rows, a_ks, a_count, t_panel):
    slots, blk = a_values.shape[2], a_values.shape[3]
    depth, width = t_panel.shape
    inner = depth // blk
    chips = nx * ny
    sub = blk // nz
    live = 64
    dma = pltpu.SemaphoreType.DMA
    any_spec = pl.BlockSpec(memory_space=pl.ANY)
    vmem_spec = pl.BlockSpec(memory_space=pltpu.VMEM)
    f32, i32, bf16 = jnp.float32, jnp.int32, jnp.bfloat16
    return pl.pallas_call(
        functools.partial(kernel, (nx, nz, ny, slots, blk, live)),
        out_shape=jax.ShapeDtypeStruct((blk, width), bf16),
        in_specs=[any_spec, vmem_spec, vmem_spec, vmem_spec, any_spec],
        out_specs=vmem_spec,
        scratch_shapes=[
            pltpu.VMEM((inner, blk, width), bf16),
            pltpu.VMEM((nz * slots, sub, blk), bf16),
            pltpu.VMEM((live, sub, blk), bf16),
            pltpu.VMEM((7, live, sub, blk), bf16),
            pltpu.VMEM((8, 128), i32),
            pltpu.VMEM((nz, 8, 128), i32),
            pltpu.VMEM((8, 128), i32),
            pltpu.SMEM((8, 128), i32),
            pltpu.VMEM((live + 1, 2 * sub, width), f32),
            pltpu.VMEM((5, chips, 2 * sub, width), f32),
            pltpu.VMEM((5, chips, 2 * sub, width), f32),
            pltpu.VMEM((5, chips, 2 * sub, width), f32),
            pltpu.VMEM((5, chips, 2 * sub, width), f32),
            pltpu.VMEM((5, chips, 2 * sub, width), f32),
            dma((3,)), dma((nz,)), dma((nz,)), dma((nz,)), dma((nz,)),
            dma((2, 4, CH)), dma((2, 4, CH)), dma((5,)), dma((5,)), dma((5, chips)), dma((5, chips)),
        ],
        compiler_params=pltpu.CompilerParams(
            collective_id=0, has_side_effects=True, vmem_limit_bytes=40 * 2**20),
        cost_estimate=pl.CostEstimate(flops=2 * live * blk * blk * width, bytes_accessed=4 * 2**20, transcendentals=0),
    )(a_values.reshape(slots, blk, blk), a_rows.reshape(1, 1, slots), a_ks.reshape(1, 1, slots), a_count,
      t_panel.reshape(inner, blk, width))


def solution(mesh):
    placed = (
        P("row", ("layer", "col"), None, None, None),
        P("row", ("layer", "col"), None),
        P("row", ("layer", "col"), None),
        P(("layer", "col"), "row"),
        P(("layer", "col"), "row"),
    )
    nx, nz, ny = mesh.shape["layer"], mesh.shape["row"], mesh.shape["col"] // 2
    return jax.shard_map(
        functools.partial(shards, nx, nz, ny),
        mesh=mesh, in_specs=placed, out_specs=P(("layer", "col"), "row"), check_vma=False
    )
```

```python
import functools

import jax
import jax.numpy as jnp
from jax import lax
from jax.experimental import pallas as pl
from jax.experimental.pallas import tpu as pltpu
from jax.sharding import PartitionSpec as P

MESH = pl.DeviceIdType.MESH
RB = 4
CH = 4


def kernel(dims, a_ref, rows_ref, ks_ref, count_ref, t_ref, out_ref,
           t_v, rxa, cmp_v, ring, meta, meta_all, tab, tab_s, run,
           mine, to_core, from_core, coded, from_chip, rows_v, ks_v, count_v,
           loc_sem, a_send, a_recv, m_send, m_recv, g_send, g_recv, c_send, c_recv, x_send, x_recv):
    nx, nz, ny, slots, blk, live = dims
    chips = nx * ny
    sub = blk // nz
    blocks = nz * RB
    lx, rz, co = lax.axis_index("layer"), lax.axis_index("row"), lax.axis_index("col")
    cy, core = lax.div(co, 2), lax.rem(co, 2)
    chip = lx * ny + cy

    def on_z(o):
        return (lx, lax.rem(rz + o + nz, nz), co)

    def on_plane(q):
        dx, dy = lax.div(q, ny), lax.rem(q, ny)
        return lax.rem(lx + dx, nx), lax.rem(cy + dy, ny)

    def plane_device(q):
        x, y = on_plane(q)
        return (x, rz, 2 * y + core)

    other_core = (lx, rz, 2 * cy + 1 - core)

    barrier = pltpu.get_barrier_semaphore()

    def greet_z(o, c_):
        pl.semaphore_signal(barrier, inc=1, device_id=on_z(o), device_id_type=MESH)
        return c_

    def greet_plane(q, c_):
        pl.semaphore_signal(barrier, inc=1, device_id=plane_device(q), device_id_type=MESH)
        return c_

    lax.fori_loop(1, nz, greet_z, 0)
    pl.semaphore_signal(barrier, inc=1, device_id=other_core, device_id_type=MESH)
    lax.fori_loop(1, chips, greet_plane, 0)

    about = [pltpu.make_async_copy(src, dst, loc_sem.at[3 + k])
             for k, (src, dst) in enumerate(((rows_ref, rows_v), (ks_ref, ks_v), (count_ref, count_v)))]
    for copy in about:
        copy.start()
    meta[...] = jnp.zeros_like(meta)
    for copy in about:
        copy.wait()
    meta[0:1, 0:slots] = rows_v[0]
    meta[1:2, 0:slots] = ks_v[0]
    meta[2:3, :] = jnp.broadcast_to(count_v[...], (1, 128))

    pl.semaphore_wait(barrier, nz - 1 + 1 + chips - 1)

    def a_copy(o):
        to = lax.rem(rz + o, nz)
        return pltpu.make_async_remote_copy(
            src_ref=a_ref.at[:, pl.ds(pl.multiple_of(to * sub, sub), sub), :],
            dst_ref=rxa.at[pl.ds(rz * slots, slots)],
            send_sem=a_send.at[0], recv_sem=a_recv.at[0], device_id=on_z(o), device_id_type=MESH)

    def m_copy(o):
        return pltpu.make_async_remote_copy(
            src_ref=meta, dst_ref=meta_all.at[rz],
            send_sem=m_send.at[0], recv_sem=m_recv.at[0], device_id=on_z(o), device_id_type=MESH)

    def start_meta(o, c_):
        m_copy(o).start()
        return c_

    def start_pieces(o, c_):
        a_copy(o).start()
        return c_

    lax.fori_loop(1, nz, start_meta, 0)
    lax.fori_loop(1, nz, start_pieces, 0)
    t_copy = pltpu.make_async_copy(t_ref, t_v, loc_sem.at[0])
    own_piece = pltpu.make_async_copy(
        a_ref.at[:, pl.ds(pl.multiple_of(rz * sub, sub), sub), :], rxa.at[pl.ds(rz * slots, slots)], loc_sem.at[1])

    own_piece.start()
    t_copy.start()

    meta_all[pl.ds(rz, 1)] = meta[...][None]

    m_all = pltpu.make_async_remote_copy(
        src_ref=meta_all.at[pl.ds(0, nz - 1)], dst_ref=meta_all.at[pl.ds(0, nz - 1)],
        send_sem=m_send.at[0], recv_sem=m_recv.at[0], device_id=other_core, device_id_type=MESH)
    m_all.wait_recv()

    row_of, col_of, count_of = meta_all[:, 0, :], meta_all[:, 1, :], meta_all[:, 2, :]
    lane = lax.broadcasted_iota(jnp.int32, (nz, 128), 1)
    group = lax.broadcasted_iota(jnp.int32, (nz, 128), 0)
    alive = lane < count_of
    row_key = jnp.where(alive, row_of, RB)
    rank = jnp.zeros((nz, 128), jnp.int32)
    in_row = jnp.zeros((nz, 128), jnp.int32)
    for g in range(nz - 1):
        rank = rank + jnp.where(group > g, jnp.broadcast_to(count_of[g:g + 1, :], (nz, 128)), 0)
    for s in range(slots):
        key = jnp.broadcast_to(row_key[:, s:s + 1], (nz, 128))
        same_before = jnp.where((key == row_key) & (lane > s), 1, 0)
        in_row = in_row + same_before
        rank = rank + same_before + jnp.where(key < row_key, 1, 0)
    rank = jnp.where(alive, rank, 1000)
    slot_at = jnp.zeros((nz, 128), jnp.int32)
    col_at = jnp.zeros((nz, 128), jnp.int32)
    keep_at = jnp.zeros((nz, 128), jnp.int32)
    upto = jnp.zeros((nz, 128), jnp.int32)
    equal = jnp.zeros((nz, 128), jnp.int32)
    for s in range(slots):
        hit = jnp.broadcast_to(rank[:, s:s + 1], (nz, 128)) == lane
        slot_at = slot_at + jnp.where(hit, group * slots + s, 0)
        col_at = col_at + jnp.where(hit, jnp.broadcast_to(col_of[:, s:s + 1], (nz, 128)), 0)
        keep_at = keep_at + jnp.where(hit, jnp.broadcast_to(in_row[:, s:s + 1], (nz, 128)), 0)
        key = jnp.broadcast_to(row_key[:, s:s + 1], (nz, 128))
        full_key = jnp.where(key < RB, group * RB + key, 1000)
        upto = upto + jnp.where(full_key <= lane, 1, 0)
        equal = equal + jnp.where(full_key == lane, 1, 0)
    last_at = jnp.sum(upto, axis=0, keepdims=True) - 1
    tab[0:1, :] = jnp.sum(slot_at, axis=0, keepdims=True)
    tab[1:2, :] = jnp.sum(col_at, axis=0, keepdims=True)
    tab[2:3, :] = jnp.sum(keep_at, axis=0, keepdims=True)
    tab[3:4, :] = jnp.where(jnp.sum(equal, axis=0, keepdims=True) > 0, last_at, live)
    tab[4:8, :] = jnp.zeros((4, 128), jnp.int32)
    table = pltpu.make_async_copy(tab, tab_s, loc_sem.at[2])
    table.start()
    run[live] = jnp.zeros(run.shape[1:], jnp.float32)
    table.wait()
    t_copy.wait()
    own_piece.wait()

    a_all = pltpu.make_async_remote_copy(
        src_ref=rxa.at[pl.ds(0, (nz - 1) * slots)], dst_ref=rxa.at[pl.ds(0, (nz - 1) * slots)],
        send_sem=a_send.at[0], recv_sem=a_recv.at[0], device_id=other_core, device_id_type=MESH)
    a_all.wait_recv()

    def compact(m, c_):
        cmp_v[m] = rxa[tab_s[0, m]]
        return c_


    cs = live // CH

    def ring_copy(d, hop, c):
        src = cmp_v if hop == 1 else ring.at[3 * d + hop - 2]
        dst = ring.at[6] if hop == 4 else ring.at[3 * d + hop - 1]
        return pltpu.make_async_remote_copy(
            src_ref=src.at[pl.ds(cs * c, cs)], dst_ref=dst.at[pl.ds(cs * c, cs)],
            send_sem=g_send.at[0], recv_sem=g_recv.at[d, hop - 1, c],
            device_id=on_z(1 - 2 * d), device_id_type=MESH)

    def last_hop_chunk(d, c):
        return (c < CH // 2) == (d == 0)

    for c in range(CH):
        lax.fori_loop(cs * c, cs * (c + 1), compact, 0, unroll=8)
        for d in (0, 1):
            ring_copy(d, 1, c).start()

    def multiply(pieces, c, carry):
        def item(i, acc):
            b = c * cs + i
            lhs = pieces[0][b] if len(pieces) == 1 else jnp.concatenate([p[b] for p in pieces], axis=0)
            term = jnp.dot(lhs, t_v[tab_s[1, b]], preferred_element_type=jnp.float32)
            acc = jnp.where(tab_s[2, b] > 0, acc, 0.0) + term
            run[b, 0:acc.shape[0]] = acc
            return acc
        return lax.fori_loop(0, cs, item, carry, unroll=8)

    def rows_in(t):
        return sub if t in (0, 4) else 2 * sub

    def core_copy(t):
        n = rows_in(t)
        return pltpu.make_async_remote_copy(
            src_ref=to_core.at[t, :, pl.ds(0, n)], dst_ref=from_core.at[t, :, pl.ds(0, n)],
            send_sem=c_send.at[0], recv_sem=c_recv.at[t], device_id=other_core, device_id_type=MESH)

    def split_rows(t):
        n = rows_in(t)

        def one(r, c_):
            mine[t, r, 0:n] = run[tab_s[3, 2 * r + core], 0:n]
            to_core[t, r, 0:n] = run[tab_s[3, 2 * r + 1 - core], 0:n]
            return c_

        lax.fori_loop(0, blocks // 2, one, 0, unroll=4)
        core_copy(t).start()

    def chip_copy(t, q):
        n = 2 * rows_in(t) + sub
        x, y = on_plane(q)
        return pltpu.make_async_remote_copy(
            src_ref=coded.at[t, x * ny + y, pl.ds(0, n)], dst_ref=from_chip.at[t, q, pl.ds(0, n)],
            send_sem=x_send.at[t], recv_sem=x_recv.at[t], device_id=(x, rz, 2 * y + core), device_id_type=MESH)

    def chips_all(t):
        n = 2 * rows_in(t) + sub
        return pltpu.make_async_remote_copy(
            src_ref=coded.at[t, pl.ds(1, chips - 1), pl.ds(0, n)], dst_ref=from_chip.at[t, pl.ds(1, chips - 1), pl.ds(0, n)],
            send_sem=x_send.at[t], recv_sem=x_recv.at[t], device_id=other_core, device_id_type=MESH)

    def send_rows(t):
        n = rows_in(t)
        core_copy(t).wait_recv()

        def one(r, c_):
            value = mine[t, r, 0:n] + from_core[t, r, 0:n]
            left, right = value[:, 0:128], value[:, 128:256]
            top = jnp.max(jnp.maximum(jnp.abs(left), jnp.abs(right)), axis=0, keepdims=True)
            power = jnp.floor(jnp.log2(jnp.maximum(top, 1e-30)) + 1.001)
            up = jnp.exp2(15.0 - power)
            for k, half in enumerate((left, right)):
                fixed = jnp.clip(jnp.round(half * up), -32767.0, 32767.0)
                coded[t, r, k * n:(k + 1) * n] = fixed.astype(jnp.int32).astype(jnp.int16)
            power = jnp.broadcast_to(power, (sub, 128))
            coded[t, r, 2 * n:2 * n + sub] = power.astype(jnp.int32).astype(jnp.int16)
            return c_

        lax.fori_loop(0, chips, one, 0, unroll=4)

        def send(q, c_):
            chip_copy(t, q).start()
            return c_

        lax.fori_loop(1, chips, send, 0)

    def finish(t):
        n = rows_in(t)

        chips_all(t).wait_recv()

        def add(q, acc):
            fixed = from_chip[t, q, 0:2 * n + sub].astype(jnp.int32).astype(jnp.float32)
            down = jnp.exp2(fixed[2 * n:2 * n + 1] - 15.0)
            return acc[0] + fixed[0:n] * down, acc[1] + fixed[n:2 * n] * down

        own = mine[t, chip, 0:n] + from_core[t, chip, 0:n]
        acc = lax.fori_loop(1, chips, add, (own[:, 0:128], own[:, 128:256]), unroll=5)
        acc = [(0.5 * half).astype(out_ref.dtype) for half in acc]
        for k in range(n // sub):
            shift = 0 if t == 0 else (t if k else nz - t)
            piece = lax.rem(rz + shift, nz)
            for h, half in enumerate(acc):
                out_ref[pl.ds(pl.multiple_of(piece * sub, sub), sub), h * 128:(h + 1) * 128] = half[k * sub:(k + 1) * sub]

    width = t_v.shape[2]
    acc = jnp.zeros((sub, width), jnp.float32)
    for c in range(CH):
        acc = multiply([cmp_v], c, acc)
    split_rows(0)
    for t in (1, 2, 3):
        acc = jnp.zeros((2 * sub, width), jnp.float32)
        for c in range(CH):
            for d in (0, 1):
                ring_copy(d, t, c).wait_recv()
                if t < 3 or last_hop_chunk(d, c):
                    ring_copy(d, t + 1, c).start()
            acc = multiply([ring.at[t - 1], ring.at[3 + t - 1]], c, acc)
            if c == 1:
                send_rows(t - 1)
        split_rows(t)
    acc = jnp.zeros((sub, width), jnp.float32)
    for c in range(CH):
        ring_copy(0 if last_hop_chunk(0, c) else 1, 4, c).wait_recv()
        acc = multiply([ring.at[6]], c, acc)
        if c == 1:
            send_rows(3)
    split_rows(4)
    for t in (0, 1, 2):
        finish(t)
    send_rows(4)
    finish(3)
    finish(4)

    m_all.wait_send()
    a_all.wait_send()
    pltpu.make_async_remote_copy(
        src_ref=ring, dst_ref=ring, send_sem=g_send.at[0], recv_sem=g_recv.at[0, 0, 0],
        device_id=other_core, device_id_type=MESH).wait_send()
    pltpu.make_async_remote_copy(
        src_ref=to_core.at[pl.ds(0, 4)], dst_ref=to_core.at[pl.ds(0, 4)], send_sem=c_send.at[0], recv_sem=c_recv.at[0],
        device_id=other_core, device_id_type=MESH).wait_send()
    for t in range(5):
        chips_all(t).wait_send()


def shards(nx, nz, ny, a_values, a_rows, a_ks, a_count, t_panel):
    slots, blk = a_values.shape[2], a_values.shape[3]
    depth, width = t_panel.shape
    inner = depth // blk
    chips = nx * ny
    sub = blk // nz
    live = 64
    dma = pltpu.SemaphoreType.DMA
    any_spec = pl.BlockSpec(memory_space=pl.ANY)
    vmem_spec = pl.BlockSpec(memory_space=pltpu.VMEM)
    f32, i32, bf16 = jnp.float32, jnp.int32, jnp.bfloat16
    return pl.pallas_call(
        functools.partial(kernel, (nx, nz, ny, slots, blk, live)),
        out_shape=jax.ShapeDtypeStruct((blk, width), bf16),
        in_specs=[any_spec] * 5,
        out_specs=vmem_spec,
        scratch_shapes=[
            pltpu.VMEM((inner, blk, width), bf16),
            pltpu.VMEM((nz * slots, sub, blk), bf16),
            pltpu.VMEM((live, sub, blk), bf16),
            pltpu.VMEM((7, live, sub, blk), bf16),
            pltpu.VMEM((8, 128), i32),
            pltpu.VMEM((nz, 8, 128), i32),
            pltpu.VMEM((8, 128), i32),
            pltpu.SMEM((8, 128), i32),
            pltpu.VMEM((live + 1, 2 * sub, width), f32),
            pltpu.VMEM((5, chips, 2 * sub, width), f32),
            pltpu.VMEM((5, chips, 2 * sub, width), f32),
            pltpu.VMEM((5, chips, 2 * sub, width), f32),
            pltpu.VMEM((5, chips, 5 * sub, 128), jnp.int16),
            pltpu.VMEM((5, chips, 5 * sub, 128), jnp.int16),
            pltpu.VMEM((1, 1, slots), i32), pltpu.VMEM((1, 1, slots), i32), pltpu.VMEM((1, 1), i32),
            dma((6,)), dma((1,)), dma((1,)), dma((1,)), dma((1,)),
            dma((1,)), dma((2, 4, CH)), dma((1,)), dma((5,)), dma((5,)), dma((5,)),
        ],
        compiler_params=pltpu.CompilerParams(
            collective_id=0, has_side_effects=True, vmem_limit_bytes=60 * 2**20),
        cost_estimate=pl.CostEstimate(flops=2 * live * blk * blk * width, bytes_accessed=4 * 2**20, transcendentals=0),
    )(a_values.reshape(slots, blk, blk), a_rows.reshape(1, 1, slots), a_ks.reshape(1, 1, slots), a_count,
      t_panel.reshape(inner, blk, width))


def solution(mesh):
    placed = (
        P("row", ("layer", "col"), None, None, None),
        P("row", ("layer", "col"), None),
        P("row", ("layer", "col"), None),
        P(("layer", "col"), "row"),
        P(("layer", "col"), "row"),
    )
    nx, nz, ny = mesh.shape["layer"], mesh.shape["row"], mesh.shape["col"] // 2
    return jax.shard_map(
        functools.partial(shards, nx, nz, ny),
        mesh=mesh, in_specs=placed, out_specs=P(("layer", "col"), "row"), check_vma=False
    )
```

```python
import functools

import jax
import jax.numpy as jnp
from jax import lax
from jax.experimental import pallas as pl
from jax.experimental.pallas import tpu as pltpu
from jax.sharding import PartitionSpec as P

MESH = pl.DeviceIdType.MESH
RB = 4
CH = 4


def kernel(dims, a_ref, meta, t_ref, out_ref,
           t_v, rxa, cmp_v, ring, meta_all, tab, tab_s, run,
           mine, to_core, from_core, coded, from_chip,
           loc_sem, a_send, a_recv, m_send, m_recv, g_send, g_recv, c_send, c_recv, x_send, x_recv):
    nx, nz, ny, slots, blk, live = dims
    chips = nx * ny
    sub = blk // nz
    blocks = nz * RB
    lx, rz, co = lax.axis_index("layer"), lax.axis_index("row"), lax.axis_index("col")
    cy, core = lax.div(co, 2), lax.rem(co, 2)
    chip = lx * ny + cy

    def on_z(o):
        return (lx, lax.rem(rz + o + nz, nz), co)

    def on_plane(q):
        dx, dy = q // ny, q % ny
        return lax.rem(lx + dx, nx), lax.rem(cy + dy, ny)

    def plane_device(q):
        x, y = on_plane(q)
        return (x, rz, 2 * y + core)

    other_core = (lx, rz, 2 * cy + 1 - core)

    far_first = sorted(range(1, chips), key=lambda q: -min(q // ny, nx - q // ny) - min(q % ny, ny - q % ny))

    barrier = pltpu.get_barrier_semaphore()

    def greet_z(o, c_):
        pl.semaphore_signal(barrier, inc=1, device_id=on_z(o), device_id_type=MESH)
        return c_

    lax.fori_loop(1, nz, greet_z, 0)
    pl.semaphore_signal(barrier, inc=1, device_id=other_core, device_id_type=MESH)
    for q in far_first:
        pl.semaphore_signal(barrier, inc=1, device_id=plane_device(q), device_id_type=MESH)

    pl.semaphore_wait(barrier, nz - 1 + 1 + chips - 1)

    def a_copy(o):
        to = lax.rem(rz + o, nz)
        return pltpu.make_async_remote_copy(
            src_ref=a_ref.at[:, pl.ds(pl.multiple_of(to * sub, sub), sub), :],
            dst_ref=rxa.at[pl.ds(rz * slots, slots)],
            send_sem=a_send.at[0], recv_sem=a_recv.at[0], device_id=on_z(o), device_id_type=MESH)

    def m_copy(o):
        return pltpu.make_async_remote_copy(
            src_ref=meta, dst_ref=meta_all.at[rz],
            send_sem=m_send.at[0], recv_sem=m_recv.at[0], device_id=on_z(o), device_id_type=MESH)

    def start_meta(o, c_):
        m_copy(o).start()
        return c_

    def start_pieces(o, c_):
        a_copy(o).start()
        return c_

    lax.fori_loop(1, nz, start_meta, 0)
    lax.fori_loop(1, nz, start_pieces, 0)
    t_copy = pltpu.make_async_copy(t_ref, t_v, loc_sem.at[0])
    own_piece = pltpu.make_async_copy(
        a_ref.at[:, pl.ds(pl.multiple_of(rz * sub, sub), sub), :], rxa.at[pl.ds(rz * slots, slots)], loc_sem.at[1])

    own_piece.start()
    t_copy.start()

    meta_all[pl.ds(rz, 1)] = meta[...][None]

    m_all = pltpu.make_async_remote_copy(
        src_ref=meta_all.at[pl.ds(0, nz - 1)], dst_ref=meta_all.at[pl.ds(0, nz - 1)],
        send_sem=m_send.at[0], recv_sem=m_recv.at[0], device_id=other_core, device_id_type=MESH)
    m_all.wait_recv()

    row_of, col_of = meta_all[:, 0, :], meta_all[:, 1, :]
    count_of = jnp.broadcast_to(meta_all[:, 2, 0:1], (nz, 128))
    lane = lax.broadcasted_iota(jnp.int32, (nz, 128), 1)
    group = lax.broadcasted_iota(jnp.int32, (nz, 128), 0)
    alive = lane < count_of
    row_key = jnp.where(alive, row_of, RB)
    rank = jnp.zeros((nz, 128), jnp.int32)
    in_row = jnp.zeros((nz, 128), jnp.int32)
    for g in range(nz - 1):
        rank = rank + jnp.where(group > g, jnp.broadcast_to(count_of[g:g + 1, :], (nz, 128)), 0)
    for s in range(slots):
        key = jnp.broadcast_to(row_key[:, s:s + 1], (nz, 128))
        same_before = jnp.where((key == row_key) & (lane > s), 1, 0)
        in_row = in_row + same_before
        rank = rank + same_before + jnp.where(key < row_key, 1, 0)
    rank = jnp.where(alive, rank, 1000)
    slot_at = jnp.zeros((nz, 128), jnp.int32)
    col_at = jnp.zeros((nz, 128), jnp.int32)
    keep_at = jnp.zeros((nz, 128), jnp.int32)
    upto = jnp.zeros((nz, 128), jnp.int32)
    equal = jnp.zeros((nz, 128), jnp.int32)
    for s in range(slots):
        hit = jnp.broadcast_to(rank[:, s:s + 1], (nz, 128)) == lane
        slot_at = slot_at + jnp.where(hit, group * slots + s, 0)
        col_at = col_at + jnp.where(hit, jnp.broadcast_to(col_of[:, s:s + 1], (nz, 128)), 0)
        keep_at = keep_at + jnp.where(hit, jnp.broadcast_to(in_row[:, s:s + 1], (nz, 128)), 0)
        key = jnp.broadcast_to(row_key[:, s:s + 1], (nz, 128))
        full_key = jnp.where(key < RB, group * RB + key, 1000)
        upto = upto + jnp.where(full_key <= lane, 1, 0)
        equal = equal + jnp.where(full_key == lane, 1, 0)
    last_at = jnp.sum(upto, axis=0, keepdims=True) - 1
    tab[0:1, :] = jnp.sum(slot_at, axis=0, keepdims=True)
    tab[1:2, :] = jnp.sum(col_at, axis=0, keepdims=True)
    tab[2:3, :] = jnp.sum(keep_at, axis=0, keepdims=True)
    tab[3:4, :] = jnp.where(jnp.sum(equal, axis=0, keepdims=True) > 0, last_at, live)
    tab[4:8, :] = jnp.zeros((4, 128), jnp.int32)
    table = pltpu.make_async_copy(tab, tab_s, loc_sem.at[2])
    table.start()
    run[live] = jnp.zeros(run.shape[1:], jnp.float32)
    table.wait()
    t_copy.wait()
    own_piece.wait()

    a_all = pltpu.make_async_remote_copy(
        src_ref=rxa.at[pl.ds(0, (nz - 1) * slots)], dst_ref=rxa.at[pl.ds(0, (nz - 1) * slots)],
        send_sem=a_send.at[0], recv_sem=a_recv.at[0], device_id=other_core, device_id_type=MESH)
    a_all.wait_recv()

    def compact(m, c_):
        cmp_v[m] = rxa[tab_s[0, m]]
        return c_


    cs = live // CH

    def ring_copy(d, hop, c):
        src = cmp_v if hop == 1 else ring.at[3 * d + hop - 2]
        dst = ring.at[6] if hop == 4 else ring.at[3 * d + hop - 1]
        return pltpu.make_async_remote_copy(
            src_ref=src.at[pl.ds(cs * c, cs)], dst_ref=dst.at[pl.ds(cs * c, cs)],
            send_sem=g_send.at[0], recv_sem=g_recv.at[d, hop - 1, c],
            device_id=on_z(1 - 2 * d), device_id_type=MESH)

    def last_hop_chunk(d, c):
        return (c < CH // 2) == (d == 0)

    for c in range(CH):
        lax.fori_loop(cs * c, cs * (c + 1), compact, 0, unroll=8)
        for d in (0, 1):
            ring_copy(d, 1, c).start()

    def multiply(pieces, c, carry):
        def item(i, acc):
            b = c * cs + i
            lhs = pieces[0][b] if len(pieces) == 1 else jnp.concatenate([p[b] for p in pieces], axis=0)
            term = jnp.dot(lhs, t_v[tab_s[1, b]], preferred_element_type=jnp.float32)
            acc = jnp.where(tab_s[2, b] > 0, acc, 0.0) + term
            run[b, 0:acc.shape[0]] = acc
            return acc
        return lax.fori_loop(0, cs, item, carry, unroll=cs)

    def rows_in(t):
        return sub if t in (0, 4) else 2 * sub

    def core_copy(t):
        n = rows_in(t)
        return pltpu.make_async_remote_copy(
            src_ref=to_core.at[t, :, pl.ds(0, n)], dst_ref=from_core.at[t, :, pl.ds(0, n)],
            send_sem=c_send.at[0], recv_sem=c_recv.at[t], device_id=other_core, device_id_type=MESH)

    def split_rows(t):
        n = rows_in(t)

        def one(r, c_):
            mine[t, r, 0:n] = run[tab_s[3, 2 * r + core], 0:n]
            to_core[t, r, 0:n] = run[tab_s[3, 2 * r + 1 - core], 0:n]
            return c_

        lax.fori_loop(0, blocks // 2, one, 0, unroll=4)
        core_copy(t).start()

    def chip_copy(t, q):
        n = 2 * rows_in(t) + sub
        x, y = on_plane(q)
        return pltpu.make_async_remote_copy(
            src_ref=coded.at[t, x * ny + y, pl.ds(0, n)], dst_ref=from_chip.at[t, q, pl.ds(0, n)],
            send_sem=x_send.at[t], recv_sem=x_recv.at[t], device_id=(x, rz, 2 * y + core), device_id_type=MESH)

    def chips_all(t):
        n = 2 * rows_in(t) + sub
        return pltpu.make_async_remote_copy(
            src_ref=coded.at[t, pl.ds(1, chips - 1), pl.ds(0, n)], dst_ref=from_chip.at[t, pl.ds(1, chips - 1), pl.ds(0, n)],
            send_sem=x_send.at[t], recv_sem=x_recv.at[t], device_id=other_core, device_id_type=MESH)

    def send_rows(t, start, stop):
        n = rows_in(t)

        for q in far_first[start:stop]:
            x, y = on_plane(q)
            r = x * ny + y
            value = mine[t, r, 0:n] + from_core[t, r, 0:n]
            left, right = value[:, 0:128], value[:, 128:256]
            top = jnp.max(jnp.maximum(jnp.abs(left), jnp.abs(right)), axis=0, keepdims=True)
            power = jnp.floor(jnp.log2(jnp.maximum(top, 1e-30)) + 1.001)
            up = jnp.exp2(15.0 - power)
            for k, half in enumerate((left, right)):
                fixed = jnp.clip(jnp.round(half * up), -32767.0, 32767.0)
                coded[t, r, k * n:(k + 1) * n] = fixed.astype(jnp.int32).astype(jnp.int16)
            power = jnp.broadcast_to(power, (sub, 128))
            coded[t, r, 2 * n:2 * n + sub] = power.astype(jnp.int32).astype(jnp.int16)
        for q in far_first[start:stop]:
            chip_copy(t, q).start()

    def finish(t):
        n = rows_in(t)

        chips_all(t).wait_recv()

        def add(q, acc):
            fixed = from_chip[t, q, 0:2 * n + sub].astype(jnp.int32).astype(jnp.float32)
            down = jnp.exp2(fixed[2 * n:2 * n + 1] - 15.0)
            return acc[0] + fixed[0:n] * down, acc[1] + fixed[n:2 * n] * down

        own = mine[t, chip, 0:n] + from_core[t, chip, 0:n]
        acc = lax.fori_loop(1, chips, add, (own[:, 0:128], own[:, 128:256]), unroll=5)
        acc = [(0.5 * half).astype(out_ref.dtype) for half in acc]
        for k in range(n // sub):
            shift = 0 if t == 0 else (t if k else nz - t)
            piece = lax.rem(rz + shift, nz)
            for h, half in enumerate(acc):
                out_ref[pl.ds(pl.multiple_of(piece * sub, sub), sub), h * 128:(h + 1) * 128] = half[k * sub:(k + 1) * sub]

    width = t_v.shape[2]
    acc = jnp.zeros((sub, width), jnp.float32)
    for c in range(CH):
        acc = multiply([cmp_v], c, acc)
    split_rows(0)
    for t in (1, 2, 3):
        acc = jnp.zeros((2 * sub, width), jnp.float32)
        for c in range(CH):
            for d in (0, 1):
                ring_copy(d, t, c).wait_recv()
                if t < 3 or last_hop_chunk(d, c):
                    ring_copy(d, t + 1, c).start()
            acc = multiply([ring.at[t - 1], ring.at[3 + t - 1]], c, acc)
            if c == 2:
                core_copy(t - 1).wait_recv()
                send_rows(t - 1, 0, chips // 2)
            if c == 3:
                send_rows(t - 1, chips // 2, chips)
        split_rows(t)
    acc = jnp.zeros((sub, width), jnp.float32)
    for c in range(CH):
        ring_copy(0 if last_hop_chunk(0, c) else 1, 4, c).wait_recv()
        acc = multiply([ring.at[6]], c, acc)
        if c == 0:
            core_copy(3).wait_recv()
            send_rows(3, 0, chips // 2)
        if c == 1:
            send_rows(3, chips // 2, chips)
    split_rows(4)
    for t in (0, 1, 2):
        finish(t)
    core_copy(4).wait_recv()
    send_rows(4, 0, chips)
    finish(3)
    finish(4)

    m_all.wait_send()
    a_all.wait_send()
    pltpu.make_async_remote_copy(
        src_ref=ring, dst_ref=ring, send_sem=g_send.at[0], recv_sem=g_recv.at[0, 0, 0],
        device_id=other_core, device_id_type=MESH).wait_send()
    pltpu.make_async_remote_copy(
        src_ref=to_core.at[pl.ds(0, 4)], dst_ref=to_core.at[pl.ds(0, 4)], send_sem=c_send.at[0], recv_sem=c_recv.at[0],
        device_id=other_core, device_id_type=MESH).wait_send()
    for t in range(5):
        chips_all(t).wait_send()


def shards(nx, nz, ny, a_values, a_rows, a_ks, a_count, t_panel):
    slots, blk = a_values.shape[2], a_values.shape[3]
    depth, width = t_panel.shape
    inner = depth // blk
    chips = nx * ny
    sub = blk // nz
    live = 64
    wide = ((0, 0), (0, 128 - slots))
    meta = jnp.concatenate([
        jnp.pad(a_rows.reshape(1, slots), wide), jnp.pad(a_ks.reshape(1, slots), wide),
        jnp.pad(a_count, ((0, 5), (0, 127)))], axis=0)
    dma = pltpu.SemaphoreType.DMA
    any_spec = pl.BlockSpec(memory_space=pl.ANY)
    vmem_spec = pl.BlockSpec(memory_space=pltpu.VMEM)
    f32, i32, bf16 = jnp.float32, jnp.int32, jnp.bfloat16
    return pl.pallas_call(
        functools.partial(kernel, (nx, nz, ny, slots, blk, live)),
        out_shape=jax.ShapeDtypeStruct((blk, width), bf16),
        in_specs=[any_spec, vmem_spec, any_spec],
        out_specs=vmem_spec,
        scratch_shapes=[
            pltpu.VMEM((inner, blk, width), bf16),
            pltpu.VMEM((nz * slots, sub, blk), bf16),
            pltpu.VMEM((live, sub, blk), bf16),
            pltpu.VMEM((7, live, sub, blk), bf16),
            pltpu.VMEM((nz, 8, 128), i32),
            pltpu.VMEM((8, 128), i32),
            pltpu.SMEM((8, 128), i32),
            pltpu.VMEM((live + 1, 2 * sub, width), f32),
            pltpu.VMEM((5, chips, 2 * sub, width), f32),
            pltpu.VMEM((5, chips, 2 * sub, width), f32),
            pltpu.VMEM((5, chips, 2 * sub, width), f32),
            pltpu.VMEM((5, chips, 5 * sub, 128), jnp.int16),
            pltpu.VMEM((5, chips, 5 * sub, 128), jnp.int16),
            dma((3,)), dma((1,)), dma((1,)), dma((1,)), dma((1,)),
            dma((1,)), dma((2, 4, CH)), dma((1,)), dma((5,)), dma((5,)), dma((5,)),
        ],
        compiler_params=pltpu.CompilerParams(
            collective_id=0, has_side_effects=True, vmem_limit_bytes=54784 * 2**10),
        cost_estimate=pl.CostEstimate(flops=2 * live * blk * blk * width, bytes_accessed=4 * 2**20, transcendentals=0),
    )(a_values.reshape(slots, blk, blk), meta, t_panel.reshape(inner, blk, width))


def solution(mesh):
    placed = (
        P("row", ("layer", "col"), None, None, None),
        P("row", ("layer", "col"), None),
        P("row", ("layer", "col"), None),
        P(("layer", "col"), "row"),
        P(("layer", "col"), "row"),
    )
    nx, nz, ny = mesh.shape["layer"], mesh.shape["row"], mesh.shape["col"] // 2
    return jax.shard_map(
        functools.partial(shards, nx, nz, ny),
        mesh=mesh, in_specs=placed, out_specs=P(("layer", "col"), "row"), check_vma=False
    )
```

```python
import functools

import jax
import jax.numpy as jnp
from jax import lax
from jax.experimental import pallas as pl
from jax.experimental.pallas import tpu as pltpu
from jax.sharding import PartitionSpec as P

MESH = pl.DeviceIdType.MESH
RB = 4
CH = 4


def kernel(dims, a_ref, meta, t_ref, out_ref,
           t_v, rxa, cmp_v, ring, meta_all, tab, tab_s, run,
           mine, to_core, from_core, coded, from_chip, step_out, step_in,
           loc_sem, a_send, a_recv, m_send, m_recv, g_send, g_recv, c_send, c_recv, x_send, x_recv, s_send, s_recv):
    nx, nz, ny, slots, blk, live = dims
    chips = nx * ny
    sub = blk // nz
    blocks = nz * RB
    lx, rz, co = lax.axis_index("layer"), lax.axis_index("row"), lax.axis_index("col")
    cy, core = lax.div(co, 2), lax.rem(co, 2)
    chip = lx * ny + cy

    def on_z(o):
        return (lx, lax.rem(rz + o + nz, nz), co)

    def on_plane(q):
        dx, dy = q // ny, q % ny
        return lax.rem(lx + dx, nx), lax.rem(cy + dy, ny)

    def plane_device(q):
        x, y = on_plane(q)
        return (x, rz, 2 * y + core)

    other_core = (lx, rz, 2 * cy + 1 - core)

    far_first = sorted(range(1, chips), key=lambda q: -min(q // ny, nx - q // ny) - min(q % ny, ny - q % ny))

    barrier = pltpu.get_barrier_semaphore()

    def greet_z(o, c_):
        pl.semaphore_signal(barrier, inc=1, device_id=on_z(o), device_id_type=MESH)
        return c_

    lax.fori_loop(1, nz, greet_z, 0)
    pl.semaphore_signal(barrier, inc=1, device_id=other_core, device_id_type=MESH)
    for q in far_first:
        pl.semaphore_signal(barrier, inc=1, device_id=plane_device(q), device_id_type=MESH)

    pl.semaphore_wait(barrier, nz - 1 + 1 + chips - 1)

    def a_copy(o):
        to = lax.rem(rz + o, nz)
        return pltpu.make_async_remote_copy(
            src_ref=a_ref.at[:, pl.ds(pl.multiple_of(to * sub, sub), sub), :],
            dst_ref=rxa.at[pl.ds(rz * slots, slots)],
            send_sem=a_send.at[0], recv_sem=a_recv.at[0], device_id=on_z(o), device_id_type=MESH)

    def m_copy(o):
        return pltpu.make_async_remote_copy(
            src_ref=meta, dst_ref=meta_all.at[rz],
            send_sem=m_send.at[0], recv_sem=m_recv.at[0], device_id=on_z(o), device_id_type=MESH)

    def start_meta(o, c_):
        m_copy(o).start()
        return c_

    def start_pieces(o, c_):
        a_copy(o).start()
        return c_

    lax.fori_loop(1, nz, start_meta, 0)
    lax.fori_loop(1, nz, start_pieces, 0)
    t_copy = pltpu.make_async_copy(t_ref, t_v, loc_sem.at[0])
    own_piece = pltpu.make_async_copy(
        a_ref.at[:, pl.ds(pl.multiple_of(rz * sub, sub), sub), :], rxa.at[pl.ds(rz * slots, slots)], loc_sem.at[1])

    own_piece.start()
    t_copy.start()

    meta_all[pl.ds(rz, 1)] = meta[...][None]

    m_all = pltpu.make_async_remote_copy(
        src_ref=meta_all.at[pl.ds(0, nz - 1)], dst_ref=meta_all.at[pl.ds(0, nz - 1)],
        send_sem=m_send.at[0], recv_sem=m_recv.at[0], device_id=other_core, device_id_type=MESH)
    m_all.wait_recv()

    row_of, col_of = meta_all[:, 0, :], meta_all[:, 1, :]
    count_of = jnp.broadcast_to(meta_all[:, 2, 0:1], (nz, 128))
    lane = lax.broadcasted_iota(jnp.int32, (nz, 128), 1)
    group = lax.broadcasted_iota(jnp.int32, (nz, 128), 0)
    alive = lane < count_of
    row_key = jnp.where(alive, row_of, RB)
    rank = jnp.zeros((nz, 128), jnp.int32)
    in_row = jnp.zeros((nz, 128), jnp.int32)
    for g in range(nz - 1):
        rank = rank + jnp.where(group > g, jnp.broadcast_to(count_of[g:g + 1, :], (nz, 128)), 0)
    for s in range(slots):
        key = jnp.broadcast_to(row_key[:, s:s + 1], (nz, 128))
        same_before = jnp.where((key == row_key) & (lane > s), 1, 0)
        in_row = in_row + same_before
        rank = rank + same_before + jnp.where(key < row_key, 1, 0)
    rank = jnp.where(alive, rank, 1000)
    slot_at = jnp.zeros((nz, 128), jnp.int32)
    col_at = jnp.zeros((nz, 128), jnp.int32)
    keep_at = jnp.zeros((nz, 128), jnp.int32)
    upto = jnp.zeros((nz, 128), jnp.int32)
    equal = jnp.zeros((nz, 128), jnp.int32)
    for s in range(slots):
        hit = jnp.broadcast_to(rank[:, s:s + 1], (nz, 128)) == lane
        slot_at = slot_at + jnp.where(hit, group * slots + s, 0)
        col_at = col_at + jnp.where(hit, jnp.broadcast_to(col_of[:, s:s + 1], (nz, 128)), 0)
        keep_at = keep_at + jnp.where(hit, jnp.broadcast_to(in_row[:, s:s + 1], (nz, 128)), 0)
        key = jnp.broadcast_to(row_key[:, s:s + 1], (nz, 128))
        full_key = jnp.where(key < RB, group * RB + key, 1000)
        upto = upto + jnp.where(full_key <= lane, 1, 0)
        equal = equal + jnp.where(full_key == lane, 1, 0)
    last_at = jnp.sum(upto, axis=0, keepdims=True) - 1
    tab[0:1, :] = jnp.sum(slot_at, axis=0, keepdims=True)
    tab[1:2, :] = jnp.sum(col_at, axis=0, keepdims=True)
    tab[2:3, :] = jnp.sum(keep_at, axis=0, keepdims=True)
    tab[3:4, :] = jnp.where(jnp.sum(equal, axis=0, keepdims=True) > 0, last_at, live)
    tab[4:8, :] = jnp.zeros((4, 128), jnp.int32)
    table = pltpu.make_async_copy(tab, tab_s, loc_sem.at[2])
    table.start()
    run[live] = jnp.zeros(run.shape[1:], jnp.float32)
    table.wait()
    t_copy.wait()
    own_piece.wait()

    a_all = pltpu.make_async_remote_copy(
        src_ref=rxa.at[pl.ds(0, (nz - 1) * slots)], dst_ref=rxa.at[pl.ds(0, (nz - 1) * slots)],
        send_sem=a_send.at[0], recv_sem=a_recv.at[0], device_id=other_core, device_id_type=MESH)
    a_all.wait_recv()

    def compact(m, c_):
        cmp_v[m] = rxa[tab_s[0, m]]
        return c_


    cs = live // CH

    def ring_copy(d, hop, c):
        src = cmp_v if hop == 1 else ring.at[3 * d + hop - 2]
        dst = ring.at[6] if hop == 4 else ring.at[3 * d + hop - 1]
        return pltpu.make_async_remote_copy(
            src_ref=src.at[pl.ds(cs * c, cs)], dst_ref=dst.at[pl.ds(cs * c, cs)],
            send_sem=g_send.at[0], recv_sem=g_recv.at[d, hop - 1, c],
            device_id=on_z(1 - 2 * d), device_id_type=MESH)

    def last_hop_chunk(d, c):
        return (c < CH // 2) == (d == 0)

    for c in range(CH):
        lax.fori_loop(cs * c, cs * (c + 1), compact, 0, unroll=8)
        for d in (0, 1):
            ring_copy(d, 1, c).start()

    def multiply(pieces, c, carry):
        def item(i, acc):
            b = c * cs + i
            lhs = pieces[0][b] if len(pieces) == 1 else jnp.concatenate([p[b] for p in pieces], axis=0)
            term = jnp.dot(lhs, t_v[tab_s[1, b]], preferred_element_type=jnp.float32)
            acc = jnp.where(tab_s[2, b] > 0, acc, 0.0) + term
            run[b, 0:acc.shape[0]] = acc
            return acc
        return lax.fori_loop(0, cs, item, carry, unroll=cs)

    def rows_in(t):
        return sub if t in (0, 4) else 2 * sub

    def core_copy(t):
        n = rows_in(t)
        return pltpu.make_async_remote_copy(
            src_ref=to_core.at[t, :, pl.ds(0, n)], dst_ref=from_core.at[t, :, pl.ds(0, n)],
            send_sem=c_send.at[0], recv_sem=c_recv.at[t], device_id=other_core, device_id_type=MESH)

    def split_rows(t):
        n = rows_in(t)

        def one(r, c_):
            mine[t, r, 0:n] = run[tab_s[3, 2 * r + core], 0:n]
            to_core[t, r, 0:n] = run[tab_s[3, 2 * r + 1 - core], 0:n]
            return c_

        lax.fori_loop(0, blocks // 2, one, 0, unroll=4)
        core_copy(t).start()

    def chip_copy(t, q):
        n = 2 * rows_in(t)
        x, y = on_plane(q)
        return pltpu.make_async_remote_copy(
            src_ref=coded.at[t, x * ny + y, pl.ds(0, n)], dst_ref=from_chip.at[t, q, pl.ds(0, n)],
            send_sem=x_send.at[t], recv_sem=x_recv.at[t], device_id=(x, rz, 2 * y + core), device_id_type=MESH)

    def step_copy(t, q):
        x, y = on_plane(q)
        return pltpu.make_async_remote_copy(
            src_ref=step_out.at[t, x * ny + y], dst_ref=step_in.at[t, q],
            send_sem=s_send.at[t], recv_sem=s_recv.at[t], device_id=(x, rz, 2 * y + core), device_id_type=MESH)

    def steps_all(t):
        return pltpu.make_async_remote_copy(
            src_ref=step_out.at[t, pl.ds(1, chips - 1)], dst_ref=step_in.at[t, pl.ds(1, chips - 1)],
            send_sem=s_send.at[t], recv_sem=s_recv.at[t], device_id=other_core, device_id_type=MESH)

    def chips_all(t):
        n = 2 * rows_in(t)
        return pltpu.make_async_remote_copy(
            src_ref=coded.at[t, pl.ds(1, chips - 1), pl.ds(0, n)], dst_ref=from_chip.at[t, pl.ds(1, chips - 1), pl.ds(0, n)],
            send_sem=x_send.at[t], recv_sem=x_recv.at[t], device_id=other_core, device_id_type=MESH)

    def send_rows(t, start, stop):
        n = rows_in(t)

        for q in far_first[start:stop]:
            x, y = on_plane(q)
            r = x * ny + y
            value = mine[t, r, 0:n] + from_core[t, r, 0:n]
            left, right = value[:, 0:128], value[:, 128:256]
            top = jnp.max(jnp.maximum(jnp.abs(left), jnp.abs(right)), axis=0, keepdims=True)
            top = jnp.maximum(top, 1e-33)
            step_out[t, r] = top * (1.0 / 32766.0)
            up = 32766.0 / top
            for k, half in enumerate((left, right)):
                coded[t, r, k * n:(k + 1) * n] = jnp.round(half * up).astype(jnp.int32).astype(jnp.int16)
        for q in far_first[start:stop]:
            step_copy(t, q).start()
            chip_copy(t, q).start()

    def finish(t):
        n = rows_in(t)

        steps_all(t).wait_recv()
        chips_all(t).wait_recv()

        def add(q, acc):
            fixed = from_chip[t, q, 0:2 * n].astype(jnp.int32).astype(jnp.float32)
            down = step_in[t, q]
            return acc[0] + fixed[0:n] * down, acc[1] + fixed[n:2 * n] * down

        own = mine[t, chip, 0:n] + from_core[t, chip, 0:n]
        acc = lax.fori_loop(1, chips, add, (own[:, 0:128], own[:, 128:256]), unroll=5)
        acc = [(0.5 * half).astype(out_ref.dtype) for half in acc]
        for k in range(n // sub):
            shift = 0 if t == 0 else (t if k else nz - t)
            piece = lax.rem(rz + shift, nz)
            for h, half in enumerate(acc):
                out_ref[pl.ds(pl.multiple_of(piece * sub, sub), sub), h * 128:(h + 1) * 128] = half[k * sub:(k + 1) * sub]

    width = t_v.shape[2]
    acc = jnp.zeros((sub, width), jnp.float32)
    for c in range(CH):
        acc = multiply([cmp_v], c, acc)
    split_rows(0)
    for t in (1, 2, 3):
        acc = jnp.zeros((2 * sub, width), jnp.float32)
        for c in range(CH):
            for d in (0, 1):
                ring_copy(d, t, c).wait_recv()
                if t < 3 or last_hop_chunk(d, c):
                    ring_copy(d, t + 1, c).start()
            acc = multiply([ring.at[t - 1], ring.at[3 + t - 1]], c, acc)
            if c == 2:
                core_copy(t - 1).wait_recv()
                send_rows(t - 1, 0, chips // 2)
            if c == 3:
                send_rows(t - 1, chips // 2, chips)
        split_rows(t)
    acc = jnp.zeros((sub, width), jnp.float32)
    for c in range(CH):
        ring_copy(0 if last_hop_chunk(0, c) else 1, 4, c).wait_recv()
        acc = multiply([ring.at[6]], c, acc)
        if c == 0:
            core_copy(3).wait_recv()
            send_rows(3, 0, chips // 2)
        if c == 1:
            send_rows(3, chips // 2, chips)
    split_rows(4)
    for t in (0, 1, 2):
        finish(t)
    core_copy(4).wait_recv()
    send_rows(4, 0, chips)
    finish(3)
    finish(4)

    m_all.wait_send()
    a_all.wait_send()
    pltpu.make_async_remote_copy(
        src_ref=ring, dst_ref=ring, send_sem=g_send.at[0], recv_sem=g_recv.at[0, 0, 0],
        device_id=other_core, device_id_type=MESH).wait_send()
    pltpu.make_async_remote_copy(
        src_ref=to_core.at[pl.ds(0, 4)], dst_ref=to_core.at[pl.ds(0, 4)], send_sem=c_send.at[0], recv_sem=c_recv.at[0],
        device_id=other_core, device_id_type=MESH).wait_send()
    for t in range(5):
        steps_all(t).wait_send()
        chips_all(t).wait_send()


def shards(nx, nz, ny, a_values, a_rows, a_ks, a_count, t_panel):
    slots, blk = a_values.shape[2], a_values.shape[3]
    depth, width = t_panel.shape
    inner = depth // blk
    chips = nx * ny
    sub = blk // nz
    live = 64
    wide = ((0, 0), (0, 128 - slots))
    meta = jnp.concatenate([
        jnp.pad(a_rows.reshape(1, slots), wide), jnp.pad(a_ks.reshape(1, slots), wide),
        jnp.pad(a_count, ((0, 5), (0, 127)))], axis=0)
    dma = pltpu.SemaphoreType.DMA
    any_spec = pl.BlockSpec(memory_space=pl.ANY)
    vmem_spec = pl.BlockSpec(memory_space=pltpu.VMEM)
    f32, i32, bf16 = jnp.float32, jnp.int32, jnp.bfloat16
    return pl.pallas_call(
        functools.partial(kernel, (nx, nz, ny, slots, blk, live)),
        out_shape=jax.ShapeDtypeStruct((blk, width), bf16),
        in_specs=[any_spec, vmem_spec, any_spec],
        out_specs=vmem_spec,
        scratch_shapes=[
            pltpu.VMEM((inner, blk, width), bf16),
            pltpu.VMEM((nz * slots, sub, blk), bf16),
            pltpu.VMEM((live, sub, blk), bf16),
            pltpu.VMEM((7, live, sub, blk), bf16),
            pltpu.VMEM((nz, 8, 128), i32),
            pltpu.VMEM((8, 128), i32),
            pltpu.SMEM((8, 128), i32),
            pltpu.VMEM((live + 1, 2 * sub, width), f32),
            pltpu.VMEM((5, chips, 2 * sub, width), f32),
            pltpu.VMEM((5, chips, 2 * sub, width), f32),
            pltpu.VMEM((5, chips, 2 * sub, width), f32),
            pltpu.VMEM((5, chips, 4 * sub, 128), jnp.int16),
            pltpu.VMEM((5, chips, 4 * sub, 128), jnp.int16),
            pltpu.VMEM((5, chips, 1, 128), f32),
            pltpu.VMEM((5, chips, 1, 128), f32),
            dma((3,)), dma((1,)), dma((1,)), dma((1,)), dma((1,)),
            dma((1,)), dma((2, 4, CH)), dma((1,)), dma((5,)), dma((5,)), dma((5,)), dma((5,)), dma((5,)),
        ],
        compiler_params=pltpu.CompilerParams(
            collective_id=0, has_side_effects=True, vmem_limit_bytes=54784 * 2**10),
        cost_estimate=pl.CostEstimate(flops=2 * live * blk * blk * width, bytes_accessed=4 * 2**20, transcendentals=0),
    )(a_values.reshape(slots, blk, blk), meta, t_panel.reshape(inner, blk, width))


def solution(mesh):
    placed = (
        P("row", ("layer", "col"), None, None, None),
        P("row", ("layer", "col"), None),
        P("row", ("layer", "col"), None),
        P(("layer", "col"), "row"),
        P(("layer", "col"), "row"),
    )
    nx, nz, ny = mesh.shape["layer"], mesh.shape["row"], mesh.shape["col"] // 2
    return jax.shard_map(
        functools.partial(shards, nx, nz, ny),
        mesh=mesh, in_specs=placed, out_specs=P(("layer", "col"), "row"), check_vma=False
    )
```

```python
import functools

import jax
import jax.numpy as jnp
from jax import lax
from jax.experimental import pallas as pl
from jax.experimental.pallas import tpu as pltpu
from jax.sharding import PartitionSpec as P

MESH = pl.DeviceIdType.MESH
RB = 4
CH = 4


def kernel(dims, a_ref, meta, t_ref, out_ref,
           t_v, rxa, cmp_v, ring, meta_all, tab, tab_s, run,
           mine, to_core, from_core, coded, from_chip, step_out, step_in,
           loc_sem, a_send, a_recv, m_send, m_recv, g_send, g_recv, c_send, c_recv, x_send, x_recv, s_send, s_recv):
    nx, nz, ny, slots, blk, live = dims
    chips = nx * ny
    sub = blk // nz
    blocks = nz * RB
    lx, rz, co = lax.axis_index("layer"), lax.axis_index("row"), lax.axis_index("col")
    cy, core = lax.div(co, 2), lax.rem(co, 2)
    chip = lx * ny + cy

    def on_z(o):
        return (lx, lax.rem(rz + o + nz, nz), co)

    def on_plane(q):
        dx, dy = q // ny, q % ny
        return lax.rem(lx + dx, nx), lax.rem(cy + dy, ny)

    def plane_device(q):
        x, y = on_plane(q)
        return (x, rz, 2 * y + core)

    other_core = (lx, rz, 2 * cy + 1 - core)

    far_first = sorted(range(1, chips), key=lambda q: -min(q // ny, nx - q // ny) - min(q % ny, ny - q % ny))

    barrier = pltpu.get_barrier_semaphore()

    def greet_z(o, c_):
        pl.semaphore_signal(barrier, inc=1, device_id=on_z(o), device_id_type=MESH)
        return c_

    lax.fori_loop(1, nz, greet_z, 0)
    pl.semaphore_signal(barrier, inc=1, device_id=other_core, device_id_type=MESH)
    for q in far_first:
        pl.semaphore_signal(barrier, inc=1, device_id=plane_device(q), device_id_type=MESH)

    pl.semaphore_wait(barrier, nz - 1 + 1 + chips - 1)

    near = 1
    far_o = range(near + 1, nz - near)
    near_o = [*range(1, near + 1), *range(nz - near, nz)]

    def a_copy(o):
        to = lax.rem(rz + o, nz)
        return pltpu.make_async_remote_copy(
            src_ref=a_ref.at[:, pl.ds(pl.multiple_of(to * sub, sub), sub), :],
            dst_ref=rxa.at[pl.ds(rz * slots, slots)],
            send_sem=a_send.at[0 if o in far_o else 1], recv_sem=a_recv.at[0], device_id=on_z(o), device_id_type=MESH)

    def m_copy(o):
        return pltpu.make_async_remote_copy(
            src_ref=meta, dst_ref=meta_all.at[rz],
            send_sem=m_send.at[0], recv_sem=m_recv.at[0], device_id=on_z(o), device_id_type=MESH)

    def start_meta(o, c_):
        m_copy(o).start()
        return c_

    lax.fori_loop(1, nz, start_meta, 0)
    for o in far_o:
        a_copy(o).start()
    t_copy = pltpu.make_async_copy(t_ref, t_v, loc_sem.at[0])
    own_piece = pltpu.make_async_copy(
        a_ref.at[:, pl.ds(pl.multiple_of(rz * sub, sub), sub), :], rxa.at[pl.ds(rz * slots, slots)], loc_sem.at[1])

    own_piece.start()
    t_copy.start()

    meta_all[pl.ds(rz, 1)] = meta[...][None]

    m_all = pltpu.make_async_remote_copy(
        src_ref=meta_all.at[pl.ds(0, nz - 1)], dst_ref=meta_all.at[pl.ds(0, nz - 1)],
        send_sem=m_send.at[0], recv_sem=m_recv.at[0], device_id=other_core, device_id_type=MESH)
    m_all.wait_recv()

    row_of, col_of = meta_all[:, 0, :], meta_all[:, 1, :]
    count_of = jnp.broadcast_to(meta_all[:, 2, 0:1], (nz, 128))
    lane = lax.broadcasted_iota(jnp.int32, (nz, 128), 1)
    group = lax.broadcasted_iota(jnp.int32, (nz, 128), 0)
    alive = lane < count_of
    row_key = jnp.where(alive, row_of, RB)
    rank = jnp.zeros((nz, 128), jnp.int32)
    in_row = jnp.zeros((nz, 128), jnp.int32)
    for g in range(nz - 1):
        rank = rank + jnp.where(group > g, jnp.broadcast_to(count_of[g:g + 1, :], (nz, 128)), 0)
    for s in range(slots):
        key = jnp.broadcast_to(row_key[:, s:s + 1], (nz, 128))
        same_before = jnp.where((key == row_key) & (lane > s), 1, 0)
        in_row = in_row + same_before
        rank = rank + same_before + jnp.where(key < row_key, 1, 0)
    rank = jnp.where(alive, rank, 1000)
    slot_at = jnp.zeros((nz, 128), jnp.int32)
    col_at = jnp.zeros((nz, 128), jnp.int32)
    keep_at = jnp.zeros((nz, 128), jnp.int32)
    upto = jnp.zeros((nz, 128), jnp.int32)
    equal = jnp.zeros((nz, 128), jnp.int32)
    for s in range(slots):
        hit = jnp.broadcast_to(rank[:, s:s + 1], (nz, 128)) == lane
        slot_at = slot_at + jnp.where(hit, group * slots + s, 0)
        col_at = col_at + jnp.where(hit, jnp.broadcast_to(col_of[:, s:s + 1], (nz, 128)), 0)
        keep_at = keep_at + jnp.where(hit, jnp.broadcast_to(in_row[:, s:s + 1], (nz, 128)), 0)
        key = jnp.broadcast_to(row_key[:, s:s + 1], (nz, 128))
        full_key = jnp.where(key < RB, group * RB + key, 1000)
        upto = upto + jnp.where(full_key <= lane, 1, 0)
        equal = equal + jnp.where(full_key == lane, 1, 0)
    last_at = jnp.sum(upto, axis=0, keepdims=True) - 1
    tab[0:1, :] = jnp.sum(slot_at, axis=0, keepdims=True)
    tab[1:2, :] = jnp.sum(col_at, axis=0, keepdims=True)
    tab[2:3, :] = jnp.sum(keep_at, axis=0, keepdims=True)
    tab[3:4, :] = jnp.where(jnp.sum(equal, axis=0, keepdims=True) > 0, last_at, live)
    tab[4:8, :] = jnp.zeros((4, 128), jnp.int32)
    table = pltpu.make_async_copy(tab, tab_s, loc_sem.at[2])
    table.start()
    run[live] = jnp.zeros(run.shape[1:], jnp.float32)
    a_sent = [pltpu.make_async_remote_copy(
        src_ref=rxa.at[pl.ds(0, k * slots)], dst_ref=rxa.at[pl.ds(0, k * slots)],
        send_sem=a_send.at[i], recv_sem=a_recv.at[0], device_id=other_core, device_id_type=MESH)
        for i, k in enumerate((len(far_o), len(near_o)))]
    a_sent[0].wait_send()
    for o in near_o:
        a_copy(o).start()
    table.wait()
    t_copy.wait()
    own_piece.wait()

    a_all = pltpu.make_async_remote_copy(
        src_ref=rxa.at[pl.ds(0, (nz - 1) * slots)], dst_ref=rxa.at[pl.ds(0, (nz - 1) * slots)],
        send_sem=a_send.at[0], recv_sem=a_recv.at[0], device_id=other_core, device_id_type=MESH)
    a_all.wait_recv()

    def compact(m, c_):
        cmp_v[m] = rxa[tab_s[0, m]]
        return c_


    cs = live // CH

    def ring_copy(d, hop, c):
        src = cmp_v if hop == 1 else ring.at[3 * d + hop - 2]
        dst = ring.at[6] if hop == 4 else ring.at[3 * d + hop - 1]
        return pltpu.make_async_remote_copy(
            src_ref=src.at[pl.ds(cs * c, cs)], dst_ref=dst.at[pl.ds(cs * c, cs)],
            send_sem=g_send.at[0], recv_sem=g_recv.at[d, hop - 1, c],
            device_id=on_z(1 - 2 * d), device_id_type=MESH)

    def last_hop_chunk(d, c):
        return (c < CH // 2) == (d == 0)

    for c in range(CH):
        lax.fori_loop(cs * c, cs * (c + 1), compact, 0, unroll=8)
        for d in (0, 1):
            ring_copy(d, 1, c).start()

    def multiply(pieces, c, carry):
        def item(i, acc):
            b = c * cs + i
            lhs = pieces[0][b] if len(pieces) == 1 else jnp.concatenate([p[b] for p in pieces], axis=0)
            term = jnp.dot(lhs, t_v[tab_s[1, b]], preferred_element_type=jnp.float32)
            acc = jnp.where(tab_s[2, b] > 0, acc, 0.0) + term
            run[b, 0:acc.shape[0]] = acc
            return acc
        return lax.fori_loop(0, cs, item, carry, unroll=cs)

    def rows_in(t):
        return sub if t in (0, 4) else 2 * sub

    def core_copy(t):
        n = rows_in(t)
        return pltpu.make_async_remote_copy(
            src_ref=to_core.at[t, :, pl.ds(0, n)], dst_ref=from_core.at[t, :, pl.ds(0, n)],
            send_sem=c_send.at[0], recv_sem=c_recv.at[t], device_id=other_core, device_id_type=MESH)

    def split_rows(t):
        n = rows_in(t)

        def one(r, c_):
            mine[t, r, 0:n] = run[tab_s[3, 2 * r + core], 0:n]
            to_core[t, r, 0:n] = run[tab_s[3, 2 * r + 1 - core], 0:n]
            return c_

        lax.fori_loop(0, blocks // 2, one, 0, unroll=4)
        core_copy(t).start()

    def chip_copy(t, q):
        n = 2 * rows_in(t)
        x, y = on_plane(q)
        return pltpu.make_async_remote_copy(
            src_ref=coded.at[t, x * ny + y, pl.ds(0, n)], dst_ref=from_chip.at[t, q, pl.ds(0, n)],
            send_sem=x_send.at[t], recv_sem=x_recv.at[t], device_id=(x, rz, 2 * y + core), device_id_type=MESH)

    def step_copy(t, q):
        x, y = on_plane(q)
        return pltpu.make_async_remote_copy(
            src_ref=step_out.at[t, x * ny + y], dst_ref=step_in.at[t, q],
            send_sem=s_send.at[t], recv_sem=s_recv.at[t], device_id=(x, rz, 2 * y + core), device_id_type=MESH)

    def steps_all(t):
        return pltpu.make_async_remote_copy(
            src_ref=step_out.at[t, pl.ds(1, chips - 1)], dst_ref=step_in.at[t, pl.ds(1, chips - 1)],
            send_sem=s_send.at[t], recv_sem=s_recv.at[t], device_id=other_core, device_id_type=MESH)

    def chips_all(t):
        n = 2 * rows_in(t)
        return pltpu.make_async_remote_copy(
            src_ref=coded.at[t, pl.ds(1, chips - 1), pl.ds(0, n)], dst_ref=from_chip.at[t, pl.ds(1, chips - 1), pl.ds(0, n)],
            send_sem=x_send.at[t], recv_sem=x_recv.at[t], device_id=other_core, device_id_type=MESH)

    def send_rows(t, start, stop):
        n = rows_in(t)

        for q in far_first[start:stop]:
            x, y = on_plane(q)
            r = x * ny + y
            value = mine[t, r, 0:n] + from_core[t, r, 0:n]
            left, right = value[:, 0:128], value[:, 128:256]
            top = jnp.max(jnp.maximum(jnp.abs(left), jnp.abs(right)), axis=0, keepdims=True)
            top = jnp.maximum(top, 1e-33)
            step_out[t, r] = top * (1.0 / 32766.0)
            up = 32766.0 / top
            for k, half in enumerate((left, right)):
                coded[t, r, k * n:(k + 1) * n] = jnp.round(half * up).astype(jnp.int32).astype(jnp.int16)
        for q in far_first[start:stop]:
            step_copy(t, q).start()
            chip_copy(t, q).start()

    def finish(t):
        n = rows_in(t)

        steps_all(t).wait_recv()
        chips_all(t).wait_recv()

        def add(q, acc):
            fixed = from_chip[t, q, 0:2 * n].astype(jnp.int32).astype(jnp.float32)
            down = step_in[t, q]
            return acc[0] + fixed[0:n] * down, acc[1] + fixed[n:2 * n] * down

        own = mine[t, chip, 0:n] + from_core[t, chip, 0:n]
        acc = lax.fori_loop(1, chips, add, (own[:, 0:128], own[:, 128:256]), unroll=5)
        acc = [(0.5 * half).astype(out_ref.dtype) for half in acc]
        for k in range(n // sub):
            shift = 0 if t == 0 else (t if k else nz - t)
            piece = lax.rem(rz + shift, nz)
            for h, half in enumerate(acc):
                out_ref[pl.ds(pl.multiple_of(piece * sub, sub), sub), h * 128:(h + 1) * 128] = half[k * sub:(k + 1) * sub]

    width = t_v.shape[2]
    acc = jnp.zeros((sub, width), jnp.float32)
    for c in range(CH):
        acc = multiply([cmp_v], c, acc)
    split_rows(0)
    for t in (1, 2, 3):
        acc = jnp.zeros((2 * sub, width), jnp.float32)
        for c in range(CH):
            for d in (0, 1):
                ring_copy(d, t, c).wait_recv()
                if t < 3 or last_hop_chunk(d, c):
                    ring_copy(d, t + 1, c).start()
            acc = multiply([ring.at[t - 1], ring.at[3 + t - 1]], c, acc)
            if c == 2:
                core_copy(t - 1).wait_recv()
                send_rows(t - 1, 0, chips // 2)
            if c == 3:
                send_rows(t - 1, chips // 2, chips)
        split_rows(t)
    acc = jnp.zeros((sub, width), jnp.float32)
    for c in range(CH):
        ring_copy(0 if last_hop_chunk(0, c) else 1, 4, c).wait_recv()
        acc = multiply([ring.at[6]], c, acc)
        if c == 0:
            core_copy(3).wait_recv()
            send_rows(3, 0, chips // 2)
        if c == 1:
            send_rows(3, chips // 2, chips)
    split_rows(4)
    for t in (0, 1, 2):
        finish(t)
    core_copy(4).wait_recv()
    send_rows(4, 0, chips)
    finish(3)
    finish(4)

    m_all.wait_send()
    a_sent[1].wait_send()
    pltpu.make_async_remote_copy(
        src_ref=ring, dst_ref=ring, send_sem=g_send.at[0], recv_sem=g_recv.at[0, 0, 0],
        device_id=other_core, device_id_type=MESH).wait_send()
    pltpu.make_async_remote_copy(
        src_ref=to_core.at[pl.ds(0, 4)], dst_ref=to_core.at[pl.ds(0, 4)], send_sem=c_send.at[0], recv_sem=c_recv.at[0],
        device_id=other_core, device_id_type=MESH).wait_send()
    for t in range(5):
        steps_all(t).wait_send()
        chips_all(t).wait_send()


def shards(nx, nz, ny, a_values, a_rows, a_ks, a_count, t_panel):
    slots, blk = a_values.shape[2], a_values.shape[3]
    depth, width = t_panel.shape
    inner = depth // blk
    chips = nx * ny
    sub = blk // nz
    live = 64
    wide = ((0, 0), (0, 128 - slots))
    meta = jnp.concatenate([
        jnp.pad(a_rows.reshape(1, slots), wide), jnp.pad(a_ks.reshape(1, slots), wide),
        jnp.pad(a_count, ((0, 5), (0, 127)))], axis=0)
    dma = pltpu.SemaphoreType.DMA
    any_spec = pl.BlockSpec(memory_space=pl.ANY)
    vmem_spec = pl.BlockSpec(memory_space=pltpu.VMEM)
    f32, i32, bf16 = jnp.float32, jnp.int32, jnp.bfloat16
    return pl.pallas_call(
        functools.partial(kernel, (nx, nz, ny, slots, blk, live)),
        out_shape=jax.ShapeDtypeStruct((blk, width), bf16),
        in_specs=[any_spec, vmem_spec, any_spec],
        out_specs=vmem_spec,
        scratch_shapes=[
            pltpu.VMEM((inner, blk, width), bf16),
            pltpu.VMEM((nz * slots, sub, blk), bf16),
            pltpu.VMEM((live, sub, blk), bf16),
            pltpu.VMEM((7, live, sub, blk), bf16),
            pltpu.VMEM((nz, 8, 128), i32),
            pltpu.VMEM((8, 128), i32),
            pltpu.SMEM((8, 128), i32),
            pltpu.VMEM((live + 1, 2 * sub, width), f32),
            pltpu.VMEM((5, chips, 2 * sub, width), f32),
            pltpu.VMEM((5, chips, 2 * sub, width), f32),
            pltpu.VMEM((5, chips, 2 * sub, width), f32),
            pltpu.VMEM((5, chips, 4 * sub, 128), jnp.int16),
            pltpu.VMEM((5, chips, 4 * sub, 128), jnp.int16),
            pltpu.VMEM((5, chips, 1, 128), f32),
            pltpu.VMEM((5, chips, 1, 128), f32),
            dma((3,)), dma((2,)), dma((1,)), dma((1,)), dma((1,)),
            dma((1,)), dma((2, 4, CH)), dma((1,)), dma((5,)), dma((5,)), dma((5,)), dma((5,)), dma((5,)),
        ],
        compiler_params=pltpu.CompilerParams(
            collective_id=0, has_side_effects=True, vmem_limit_bytes=54784 * 2**10),
        cost_estimate=pl.CostEstimate(flops=2 * live * blk * blk * width, bytes_accessed=4 * 2**20, transcendentals=0),
    )(a_values.reshape(slots, blk, blk), meta, t_panel.reshape(inner, blk, width))


def solution(mesh):
    placed = (
        P("row", ("layer", "col"), None, None, None),
        P("row", ("layer", "col"), None),
        P("row", ("layer", "col"), None),
        P(("layer", "col"), "row"),
        P(("layer", "col"), "row"),
    )
    nx, nz, ny = mesh.shape["layer"], mesh.shape["row"], mesh.shape["col"] // 2
    return jax.shard_map(
        functools.partial(shards, nx, nz, ny),
        mesh=mesh, in_specs=placed, out_specs=P(("layer", "col"), "row"), check_vma=False
    )
```
